512 devices in a mesh: row: 16 (over x, z_lo), col: 32 (over y, z_hi, core).
Axes of the slice: x: 4, y: 4, z: 16 (z_hi: 4, z_lo: 4; z = z_hi * 4 + z_lo), core: 2. Of those that a mesh axis runs over, the one named last changes fastest.
Arguments:
- attn: bfloat16 [2048, 16384], P('col', 'row'), may hold values from -6 to 6
- w_out: bfloat16 [16384, 16384], P('row', 'col'), may hold values from -0.046875 to 0.046875
- resid: bfloat16 [2048, 16384], P('row', 'col'), may hold values from -6 to 6
- gain: float32 [16384], P('col'), may hold values from 0.3 to 3
Outputs:
- stream: bfloat16 [2048, 16384], P('row', 'col')
- gram: float32 [16384, 16384], P('row', 'col')
The draws below stay inside these ranges and needn't reach their ends.
All inputs are finite; a program needn't handle non-finite values.
Results may differ from the reference program's by a relative error of at most 0.0034.
Values may be sent and summed in bfloat16 or wider, within the bound.
A program may use at most 64 MiB of HBM per device.

```python
import math
import jax
import jax.numpy as jnp
from jax import lax

D = 16384
TOKENS = 2048
N_ROW = 16


def shard_levels(stream_key, extent, split, least, high):
    level, own = 1.0, jax.random.fold_in(stream_key, 6)
    for axis_at, parts in split:
        draws = jnp.exp(jax.random.uniform(jax.random.fold_in(own, axis_at), (parts,), jnp.float32, least / len(split), high / len(split)))
        level = level * jnp.repeat(draws, extent[axis_at] // parts).reshape([-1 if axis == axis_at else 1 for axis in range(len(extent))])
    return level


def normal_values(own_key, shape, spread, bound, split=(), held_as=jnp.bfloat16):
    values = jax.random.normal(own_key, shape, jnp.float32) * spread
    if len(split) > 0:
        values = shard_levels(own_key, shape, split, -0.22, 0.18) * values
    return jnp.clip(values, min=-bound, max=bound).astype(held_as)


def setup_inputs(seed: int = 0) -> dict:
    streams_of = jax.random.split(jax.random.key(seed), 5)
    attn = normal_values(streams_of[0], (TOKENS, D), 1.0, 6.0, ((0, 32), (1, 16)))
    w_out = normal_values(streams_of[1], (D, D), D ** -0.5, 0.046875, ((0, 16), (1, 32)))
    resid = normal_values(streams_of[2], (TOKENS, D), 1.0, 6.0, ((0, 16), (1, 32)))
    gain = jnp.clip(jnp.exp(math.log(3.0) - 2.3025851 * jax.random.uniform(streams_of[3], (D,), jnp.float32) ** shard_levels(streams_of[3], (D,), ((0, 32),), -0.2, 0.2)), 0.3, 3.0)
    return {"attn": attn, "w_out": w_out, "resid": resid, "gain": gain}


def reference(attn, w_out, resid, gain):
    proj = jnp.dot(attn, w_out, preferred_element_type=jnp.float32)
    summed = resid.astype(jnp.float32) + proj
    stream = summed.astype(jnp.bfloat16)
    squares = lax.optimization_barrier(jnp.sum(summed * summed, axis=1, keepdims=True))
    normed = (summed * gain[None, :] * lax.rsqrt(squares / D + 1e-05)).astype(jnp.bfloat16)
    block_rows = D // N_ROW
    starts = jnp.arange(N_ROW, dtype=jnp.int32) * block_rows

    def one_block(start):
        left = lax.dynamic_slice_in_dim(normed, start, block_rows, 1)
        tile = lax.dot_general(left, normed, (((0,), (0,)), ((), ())), preferred_element_type=jnp.float32)
        tile = tile * (2.0 / TOKENS)
        rows_idx = start + jnp.arange(block_rows, dtype=jnp.int32)[:, None]
        cols_idx = jnp.arange(D, dtype=jnp.int32)[None, :]
        return jnp.where(cols_idx >= rows_idx, tile, jnp.zeros_like(tile))
    gram = lax.map(one_block, starts).reshape(D, D)
    return (stream, gram)
```

```python
import jax
import jax.numpy as jnp
from jax import lax
from jax.experimental import pallas as pl
from jax.experimental.pallas import tpu as pltpu
from jax.sharding import PartitionSpec as P

D = 16384
TOKENS = 2048
EPS = 1e-05
MESH = pl.DeviceIdType.MESH
F32 = jnp.float32
BF16 = jnp.bfloat16
ORDER = (0, 1, 3, 2)


def device(x, zl, y, zh, k):
    return (x * 4 + zl, (y * 4 + zh) * 2 + k)


def kernel(
    attn, w_out, resid, gain,
    stream, gram,
    A, W, XS, XR, ACC, ZS, ZR, RB, G, SUM, S2, SR, SQS, SQ, N, M, C, CS, R,
    loc, ks, kr, zs, zr, ys, yr, xs, xr, ls, lr, qs, qr, ms, mr, hs, hr,
    vs, vr, cs, cr, es, er,
):
    row, col = lax.axis_index("row"), lax.axis_index("col")
    x, zl = row // 4, row % 4
    y, zh, k = col // 8, (col // 2) % 4, col % 2
    other = 1 - k

    def at(dx=0, dl=0, dy=0, dh=0):
        return device((x + dx) % 4, (zl + dl) % 4, (y + dy) % 4, (zh + dh) % 4, k)

    sibling = device(x, zl, y, zh, other)
    sends = []

    def copy(src, dst, ssem, rsem, to):
        return pltpu.make_async_remote_copy(
            src_ref=src, dst_ref=dst, send_sem=ssem, recv_sem=rsem,
            device_id=to, device_id_type=MESH,
        )

    def send(src, dst, ssem, rsem, to, when=None):
        c = copy(src, dst, ssem, rsem, to)
        if when is None:
            c.start()
        else:
            pl.when(when)(c.start)
        sends.append((c, when))

    def arrived(dst, ssem, rsem, when=None):
        c = copy(dst, dst, ssem, rsem, sibling)
        if when is None:
            c.wait_recv()
        else:
            pl.when(when)(c.wait_recv)

    bar = pltpu.get_barrier_semaphore()

    def greet(dev, when=None):
        def go():
            pl.semaphore_signal(bar, inc=1, device_id=dev, device_id_type=MESH)
        if when is None:
            go()
        else:
            pl.when(when)(go)

    greet(sibling)
    for d in range(1, 4):
        greet(at(dx=d))
        greet(at(dl=d))
    for dy in range(4):
        for dh in range(4):
            if dy or dh:
                greet(at(dy=dy, dh=dh))
    for s in range(4):
        greet(device(s, zl, x, zh, k), jnp.logical_or(x != y, x != s))
        greet(device(x, s, y, zl, k), jnp.logical_or(zl != zh, zl != s))
    pl.semaphore_wait(
        bar, 22 + 8 - (x == y).astype(jnp.int32) - (zl == zh).astype(jnp.int32)
    )

    for d in (1, 3, 2):
        send(attn, A.at[y, zh], zs.at[d], zr.at[d], at(dh=d))
    for d in (1, 3, 2):
        send(attn, A.at[y, zh], ys.at[0, d], yr.at[0, d], at(dy=d))
    own_w = pltpu.make_async_copy(w_out, W.at[k], loc.at[0])
    own_w.start()
    send(w_out, W.at[k], ks.at[0], kr.at[0], sibling)
    off_other = pl.multiple_of(other * 64, 64)
    off_mine = pl.multiple_of(k * 64, 64)
    send(resid.at[pl.ds(off_other, 64)], RB.at[k], ks.at[1], kr.at[1], sibling)
    send(gain, G.at[k], ks.at[2], kr.at[2], sibling)
    A[y, zh] = attn[...]
    RB[k] = resid[pl.ds(off_mine, 64), :]
    G[k] = gain[...]
    own_w.wait()
    arrived(W.at[other], ks.at[0], kr.at[0])

    def project(i, jz):
        zp = (zh + 4 - jz) % 4

        @pl.loop(0, 4)
        def _(jy):
            yp = (y + 4 - jy) % 4

            @pl.when(jy > 0)
            def _():
                arrived(A.at[yp, zp], ys.at[jz, jy], yr.at[jz, jy])

            for h in range(2):
                part = jnp.dot(A[yp, zp], W[h], preferred_element_type=F32)
                XS[yp, zp, :, h * 512:(h + 1) * 512] = part.astype(BF16)

                @pl.when(yp == x)
                def _():
                    ACC[zp, :, h * 512:(h + 1) * 512] = part

            @pl.when(yp != x)
            def _():
                copy(
                    XS.at[yp, zp], XR.at[x, zp], xs.at[jy, jz], xr.at[x, jz],
                    device(yp, zl, y, zh, k),
                ).start()

    def combine(jz):
        zp = (zh + 4 - jz) % 4
        total = ACC[zp]
        for d in range(1, 4):
            src = (x + d) % 4
            arrived(XR.at[src, zp], xs.at[0, 0], xr.at[src, jz])
            total = total + XR[src, zp].astype(F32)

        @pl.when(zp == zl)
        def _():
            SUM[...] = total

        @pl.when(zp != zl)
        def _():
            ZS[zp] = total.astype(BF16)
            copy(
                ZS.at[zp], ZR.at[zl], ls.at[jz], lr.at[zl], device(x, zp, y, zh, k)
            ).start()

    project(0, 0)
    for jz in (1, 3, 2):
        zp = (zh + 4 - jz) % 4
        arrived(A.at[y, zp], zs.at[jz], zr.at[jz])
        for d in (1, 3, 2):
            send(A.at[y, zp], A.at[y, zp], ys.at[jz, d], yr.at[jz, d], at(dy=d))
    project(1, 1)
    combine(0)
    project(2, 3)
    combine(1)
    project(3, 2)
    combine(3)
    combine(2)

    arrived(RB.at[other], ks.at[1], kr.at[1])
    arrived(G.at[other], ks.at[2], kr.at[2])
    for d in range(1, 4):
        src = (zl + d) % 4
        arrived(ZR.at[src], ls.at[0], lr.at[src])
    squares = jnp.zeros((64, 1), F32)
    for h in range(2):
        part = slice(h * 512, (h + 1) * 512)
        total = SUM[:, part]
        for d in range(1, 4):
            total = total + ZR[(zl + d) % 4, :, part].astype(F32)
        total = total + RB[h].astype(F32)
        SUM[:, part] = total
        S2[h] = total.astype(BF16)
        squares = squares + jnp.sum(total * total, axis=1, keepdims=True)
    wide = jnp.concatenate(
        [jnp.broadcast_to(squares, (64, 128)), jnp.zeros((64, 128), F32)], axis=0
    )
    flat = wide.T
    SQS[...] = flat[0:8]
    for dy in range(4):
        for dh in range(4):
            if dy or dh:
                i = dy * 4 + dh
                send(SQS, SQ.at[i], qs.at[i], qr.at[i], at(dy=dy, dh=dh))
    send(S2.at[other], SR, ks.at[3], kr.at[3], sibling)
    stream[pl.ds(off_mine, 64), :] = S2[k]
    total = SQS[...]
    for i in range(1, 16):
        arrived(SQ.at[i], qs.at[i], qr.at[i])
        total = total + SQ[i]
    scale = lax.rsqrt(total / D + EPS)
    scale = jnp.broadcast_to(scale[0:1], (128, 128)).T[0:64, 0:1]
    for h in range(2):
        part = slice(h * 512, (h + 1) * 512)
        normed = SUM[:, part] * G[h] * scale
        N[h] = normed.astype(BF16).reshape(4, 16, 512)

    for q in range(4):
        away = jnp.logical_or(x != y, y != q)
        send(N.at[:, q], M.at[:, x], ms.at[q], mr.at[x], device(y, zl, q, zh, k), away)
    for d in (1, 3, 2):
        send(N, C.at[:, :, zl, x], hs.at[d], hr.at[d], at(dl=d))
    for d in (1, 3, 2):
        send(N, C.at[:, :, zl, x], cs.at[0, d], cr.at[0, d], at(dx=d))

    @pl.when(x == y)
    def _():
        for h in range(2):
            M[h, x] = N[h, y]

    for h in range(2):
        for q in range(4):
            C[h, q, zl, x] = N[h, q]
    for s in range(4):
        arrived(M.at[:, s], ms.at[0], mr.at[s], jnp.logical_or(x != y, x != s))
    for j in range(4):
        away = jnp.logical_or(zl != zh, zh != j)
        send(M, R.at[k, y, zl], vs.at[j], vr.at[zl], device(x, zh, y, j, k), away)

    @pl.when(zl == zh)
    def _():
        R[k, y, zl] = M[...]

    for dl in (1, 3, 2):
        lp = (zl + 4 - dl) % 4
        arrived(C.at[:, :, lp, x], hs.at[dl], hr.at[dl])
        for d in (1, 3, 2):
            piece = C.at[:, :, lp, x]
            send(piece, piece, cs.at[dl, d], cr.at[dl, d], at(dx=d))
    for s in range(4):
        arrived(R.at[k, y, s], vs.at[0], vr.at[s], jnp.logical_or(zl != zh, zl != s))
        for d in (1, 3, 2):
            piece = R.at[k, y, s]
            send(piece, piece, es.at[s, d], er.at[s, d], at(dy=d))
    send(R.at[k, y], R.at[k, y], ks.at[4], kr.at[4], sibling)
    for dl in range(4):
        for dx in range(1, 4):
            piece = C.at[:, :, (zl + 4 - dl) % 4, (x + 4 - dx) % 4]
            arrived(piece, cs.at[dl, dx], cr.at[dl, dx])
    send(C.at[other], CS, ks.at[8], kr.at[8], sibling)
    arrived(SR, ks.at[3], kr.at[3])
    stream[pl.ds(off_other, 64), :] = SR[...]
    arrived(CS, ks.at[8], kr.at[8])

    def accumulate(q, first, last):
        @pl.loop(0, 2)
        def _(h):
            for half in range(2):
                lanes = slice(half * 256, (half + 1) * 256)
                tile = None
                for lane, rhs in ((k, C.at[k]), (other, CS)):
                    left = R[lane, q, :, h, :, :, lanes].reshape(256, 256)
                    right = rhs[q].reshape(256, 512)
                    term = lax.dot_general(
                        left, right, (((0,), (0,)), ((), ())),
                        preferred_element_type=F32,
                    )
                    tile = term if tile is None else tile + term
                start = pl.multiple_of(h * 512 + half * 256, 256)
                rows = pl.ds(start, 256)
                if not first:
                    tile = tile + gram[rows, :]
                if last:
                    tile = tile * (2.0 / TOKENS)
                    rid = row * 1024 + start + lax.broadcasted_iota(
                        jnp.int32, (256, 512), 0
                    )
                    cid = col * 512 + lax.broadcasted_iota(jnp.int32, (256, 512), 1)
                    tile = jnp.where(cid >= rid, tile, 0.0)
                gram[rows, :] = tile

    for jy in range(4):
        q = (y + 4 - jy) % 4
        if jy:
            for s in range(4):
                arrived(R.at[k, q, s], es.at[s, jy], er.at[s, jy])
            send(R.at[k, q], R.at[k, q], ks.at[4 + jy], kr.at[4 + jy], sibling)
        arrived(R.at[other, q], ks.at[4 + jy], kr.at[4 + jy])
        accumulate(q, jy == 0, jy == 3)

    for c, when in sends:
        if when is None:
            c.wait_send()
        else:
            pl.when(when)(c.wait_send)
    for jz in range(4):
        zp = (zh + 4 - jz) % 4
        for jy in range(4):
            yp = (y + 4 - jy) % 4
            c = copy(
                XS.at[yp, zp], XR.at[x, zp], xs.at[jy, jz], xr.at[x, jz],
                device(yp, zl, y, zh, k),
            )
            pl.when(yp != x)(c.wait_send)
        c = copy(ZS.at[zp], ZR.at[zl], ls.at[jz], lr.at[zl], device(x, zp, y, zh, k))
        pl.when(zp != zl)(c.wait_send)


def local(attn, w_out, resid, gain):
    dma = pltpu.SemaphoreType.DMA
    vmem = pltpu.VMEM
    whole = pl.BlockSpec(memory_space=pltpu.VMEM)
    return pl.pallas_call(
        kernel,
        out_shape=(
            jax.ShapeDtypeStruct((128, 512), BF16),
            jax.ShapeDtypeStruct((1024, 512), F32),
        ),
        in_specs=[whole, pl.BlockSpec(memory_space=pl.ANY), whole, whole],
        out_specs=(whole, whole),
        scratch_shapes=[
            vmem((4, 4, 64, 1024), BF16),
            vmem((2, 1024, 512), BF16),
            vmem((4, 4, 64, 1024), BF16),
            vmem((4, 4, 64, 1024), BF16),
            vmem((4, 64, 1024), F32),
            vmem((4, 64, 1024), BF16),
            vmem((4, 64, 1024), BF16),
            vmem((2, 64, 512), BF16),
            vmem((2, 1, 512), F32),
            vmem((64, 1024), F32),
            vmem((2, 64, 512), BF16),
            vmem((64, 512), BF16),
            vmem((8, 128), F32),
            vmem((16, 8, 128), F32),
            vmem((2, 4, 16, 512), BF16),
            vmem((2, 4, 16, 512), BF16),
            vmem((2, 4, 4, 4, 16, 512), BF16),
            vmem((4, 4, 4, 16, 512), BF16),
            vmem((2, 4, 4, 2, 4, 16, 512), BF16),
            dma((1,)), dma((9,)), dma((9,)), dma((4,)), dma((4,)),
            dma((4, 4)), dma((4, 4)), dma((4, 4)), dma((4, 4)),
            dma((4,)), dma((4,)), dma((16,)), dma((16,)), dma((4,)), dma((4,)),
            dma((4,)), dma((4,)), dma((4,)), dma((4,)), dma((4, 4)), dma((4, 4)),
            dma((4, 4)), dma((4, 4)),
        ],
        compiler_params=pltpu.CompilerParams(
            collective_id=0, has_side_effects=True, vmem_limit_bytes=48 << 20
        ),
        cost_estimate=pl.CostEstimate(
            flops=4 * 2048 * 1024 * 512, bytes_accessed=16 << 20, transcendentals=128
        ),
    )(attn, w_out, resid, gain.reshape(1, 512))


def solution(mesh):
    placed = (P("col", "row"), P("row", "col"), P("row", "col"), P("col"))
    return jax.shard_map(
        local,
        mesh=mesh,
        in_specs=placed,
        out_specs=(P("row", "col"), P("row", "col")),
        check_vma=False,
    )
```

```python
import jax
import jax.numpy as jnp
from jax import lax
from jax.experimental import pallas as pl
from jax.experimental.pallas import tpu as pltpu
from jax.sharding import PartitionSpec as P

D = 16384
TOKENS = 2048
EPS = 1e-05
MESH = pl.DeviceIdType.MESH
F32 = jnp.float32
BF16 = jnp.bfloat16
PARTS = 4
T = 64 // PARTS
AHEAD = 2
STEPS = (
    ("attention_z", 36, 5), ("attention_y", 40, 5), ("project", 47, 6),
    ("combine", 55, 6.5), ("squares", 61, 6.5), ("norm", 66, 6.5),
    ("multicast", 70, 7), ("rows_z", 75, 7), ("rows_y", 80, 7), ("rows_core", 88, 7),
    ("gram", 91, 7),
)


def device(x, zl, y, zh, k):
    return (x * 4 + zl, (y * 4 + zh) * 2 + k)


def kernel(
    attn, w_out, resid, gain,
    stream, gram,
    A, W, XS, XR, ACC, ZS, ZR, RB, G, SUM, S2, SR, SQS, SQ, N, M, C, CS, R,
    loc, ks, kr, zs, zr, ys, yr, xs, xr, ls, lr, qs, qr, ms, mr, hs, hr,
    vs, vr, cs, cr, es, er, fs, fr, gs, gr, ts,
):
    row, col = lax.axis_index("row"), lax.axis_index("col")
    x, zl = row // 4, row % 4
    y, zh, k = col // 8, (col // 2) % 4, col % 2
    other = 1 - k

    def at(dx=0, dl=0, dy=0, dh=0):
        return device((x + dx) % 4, (zl + dl) % 4, (y + dy) % 4, (zh + dh) % 4, k)

    sibling = device(x, zl, y, zh, other)
    sends = []

    def copy(src, dst, ssem, rsem, to):
        return pltpu.make_async_remote_copy(
            src_ref=src, dst_ref=dst, send_sem=ssem, recv_sem=rsem,
            device_id=to, device_id_type=MESH,
        )

    def send(src, dst, ssem, rsem, to, when=None):
        c = copy(src, dst, ssem, rsem, to)
        if when is None:
            c.start()
        else:
            pl.when(when)(c.start)
        sends.append((c, when))

    def arrived(dst, ssem, rsem, when=None):
        c = copy(dst, dst, ssem, rsem, sibling)
        if when is None:
            c.wait_recv()
        else:
            pl.when(when)(c.wait_recv)

    off_other = pl.multiple_of(other * 64, 64)
    off_mine = pl.multiple_of(k * 64, 64)
    own = [
        pltpu.make_async_copy(w_out, W.at[k], loc.at[0]),
        pltpu.make_async_copy(resid.at[pl.ds(off_mine, 64)], RB.at[k], loc.at[1]),
        pltpu.make_async_copy(gain, G.at[k], loc.at[2]),
    ] + [
        pltpu.make_async_copy(attn.at[pl.ds(c * T, T)], A.at[c, y, zh], loc.at[3 + c])
        for c in range(PARTS)
    ]
    for c in own:
        c.start()

    bar = pltpu.get_barrier_semaphore()

    def greet(dev, when=None):
        def go():
            pl.semaphore_signal(bar, inc=1, device_id=dev, device_id_type=MESH)
        if when is None:
            go()
        else:
            pl.when(when)(go)

    greet(sibling)
    for d in range(1, 4):
        greet(at(dx=d))
        greet(at(dl=d))
    for dy in range(4):
        for dh in range(4):
            if dy or dh:
                greet(at(dy=dy, dh=dh))
    for s in range(4):
        greet(device(s, zl, x, zh, k), jnp.logical_or(x != y, x != s))
        greet(device(x, s, y, zl, k), jnp.logical_or(zl != zh, zl != s))
    pl.semaphore_wait(
        bar, 22 + 8 - (x == y).astype(jnp.int32) - (zl == zh).astype(jnp.int32)
    )

    def attention_out(c):
        for d in (1, 3):
            send(
                attn.at[pl.ds(c * T, T)], A.at[c, y, zh], zs.at[c, d], zr.at[c, d],
                at(dh=d),
            )

    for c in range(AHEAD):
        attention_out(c)
    send(w_out, W.at[k], ks.at[0], kr.at[0], sibling)
    send(resid.at[pl.ds(off_other, 64)], RB.at[k], ks.at[1], kr.at[1], sibling)
    send(gain, G.at[k], ks.at[2], kr.at[2], sibling)
    for c in own:
        c.wait()
    arrived(W.at[other], ks.at[0], kr.at[0])
    arrived(RB.at[other], ks.at[1], kr.at[1])
    arrived(G.at[other], ks.at[2], kr.at[2])

    def to_x(c, yp):
        return copy(
            XS.at[c, yp], XR.at[c, x], xs.at[c, yp], xr.at[c, x],
            device(yp, zl, y, zh, k),
        )

    def to_zl(c, zp):
        return copy(
            ZS.at[c, zp], ZR.at[c, zl], ls.at[c, zp], lr.at[c, zl],
            device(x, zp, y, zh, k),
        )

    def project_block(c, yp):
        left = A[c, yp].reshape(4 * T, 1024)
        for h in range(2):
            lanes = slice(h * 512, (h + 1) * 512)
            part = jnp.dot(left, W[h], preferred_element_type=F32).reshape(4, T, 512)

            @pl.when(yp == x)
            def _():
                ACC[c, :, :, lanes] = part

            @pl.when(yp != x)
            def _():
                XS[c, yp, :, :, lanes] = part.astype(BF16)

        pl.when(yp != x)(lambda: to_x(c, yp).start())

    def attention_z(c):
        d = 1 if c % 2 == 0 else 3
        piece = A.at[c, y, (zh + 4 - d) % 4]
        arrived(piece, zs.at[c, d], zr.at[c, d])
        send(piece, piece, zs.at[c, 2], zr.at[c, 2], at(dh=d))
        if c + AHEAD < PARTS:
            attention_out(c + AHEAD)

    def attention_y(c):
        for d in ((3, 2) if c % 2 == 0 else (1, 2)):
            arrived(A.at[c, y, (zh + 4 - d) % 4], zs.at[c, d], zr.at[c, d])
        for d in (1, 3, 2):
            send(A.at[c, y], A.at[c, y], ys.at[c, d], yr.at[c, d], at(dy=d))
        project_block(c, y)

    def project(c):
        @pl.loop(1, 4)
        def _(d):
            yp = (y + 4 - d) % 4
            arrived(A.at[c, yp], ys.at[c, d], yr.at[c, d])
            project_block(c, yp)

    def combine(c):
        total = ACC[c]
        for d in range(1, 4):
            src = (x + d) % 4
            arrived(XR.at[c, src], xs.at[c, 0], xr.at[c, src])
            total = total + XR[c, src].astype(F32)
        ACC[c] = total
        ZS[c] = total.astype(BF16)
        for d in (1, 3, 2):
            to_zl(c, (zl + d) % 4).start()

    def squares(c):
        rows = slice(c * T, (c + 1) * T)
        for d in range(1, 4):
            src = (zl + d) % 4
            arrived(ZR.at[c, src], ls.at[c, 0], lr.at[c, src])
        summed_squares = jnp.zeros((T, 1), F32)
        for h in range(2):
            lanes = slice(h * 512, (h + 1) * 512)
            total = ACC[c, zl, :, lanes]
            for d in range(1, 4):
                total = total + ZR[c, (zl + d) % 4, :, lanes].astype(F32)
            total = total + RB[h, rows, :].astype(F32)
            SUM[c, :, lanes] = total
            S2[h, rows, :] = total.astype(BF16)
            summed_squares = summed_squares + jnp.sum(total * total, axis=1, keepdims=True)
        wide = jnp.concatenate(
            [
                jnp.broadcast_to(summed_squares, (T, 128)),
                jnp.zeros((128 - T, 128), F32),
            ],
            axis=0,
        )
        SQS[c] = wide.T[0:1]
        for dh in (2, 1, 3, 0):
            for dy in (2, 1, 3, 0):
                if dy or dh:
                    i = dy * 4 + dh
                    send(
                        SQS.at[c], SQ.at[c, i], qs.at[c, i], qr.at[c, i],
                        at(dy=dy, dh=dh),
                    )
        if c == PARTS - 1:
            send(S2.at[other], SR, ks.at[3], kr.at[3], sibling)

    def norm(c):
        total = SQS[c]
        for i in range(1, 16):
            arrived(SQ.at[c, i], qs.at[c, i], qr.at[c, i])
            total = total + SQ[c, i]
        scale = lax.rsqrt(total / D + EPS)
        scale = jnp.broadcast_to(scale, (128, 128)).T[0:T, 0:1]
        for f in range(4):
            lanes = slice(f * 256, (f + 1) * 256)
            g = G[f // 2, :, (f % 2) * 256:(f % 2) * 256 + 256]
            normed = (SUM[c, :, lanes] * g * scale).astype(BF16)
            N[c, f] = normed
            C[c, zl, x, f] = normed

        @pl.when(x == y)
        def _():
            M[c, x] = N[c, y]

        for q in range(4):
            away = jnp.logical_or(x != y, y != q)
            send(
                N.at[c, q], M.at[c, x], ms.at[c, q], mr.at[c, x],
                device(y, zl, q, zh, k), away,
            )
        for d in (1, 3, 2):
            send(N.at[c], C.at[c, zl, x], hs.at[c, d], hr.at[c, d], at(dl=d))

    def multicast(c):
        for s in range(4):
            arrived(
                M.at[c, s], ms.at[c, 0], mr.at[c, s], jnp.logical_or(x != y, x != s)
            )
        up = (zh + (zl > zh).astype(jnp.int32)) % 4
        for i, (j, away) in enumerate(((up, zl != zh), ((up + 3) % 4, None))):
            send(
                M.at[c], R.at[k, c, y, zl], vs.at[c, i], vr.at[c, zl],
                device(x, zh, y, j, k), away,
            )

        @pl.when(zl == zh)
        def _():
            R[k, c, y, zl] = M[c]

        for d in (1, 3, 2):
            arrived(C.at[c, (zl + 4 - d) % 4, x], hs.at[c, d], hr.at[c, d])
        for d in (1, 3, 2):
            piece = C.at[c, :, x]
            send(piece, piece, cs.at[c, d], cr.at[c, d], at(dx=d))

    def direct(s):
        up = (zl + (zl < s).astype(jnp.int32)) % 4
        return zh == up, zh == (up + 3) % 4

    def rows_z(c):
        for s in range(4):
            above, below = direct(s)
            piece = R.at[k, c, y, s]
            first = jnp.logical_or(above, below)
            here = jnp.logical_and(zl == zh, zl == s)
            arrived(
                piece, vs.at[c, 0], vr.at[c, s],
                jnp.logical_and(first, jnp.logical_not(here)),
            )
            to = jnp.where(above, 1, 3)
            send(piece, piece, ts.at[c, s], vr.at[c, s], at(dh=to), first)

    def rows_y(c):
        piece = R.at[k, c, y]
        for s in range(4):
            above, below = direct(s)
            arrived(
                R.at[k, c, y, s], vs.at[c, 0], vr.at[c, s],
                jnp.logical_not(jnp.logical_or(above, below)),
            )
        for d in (1, 3, 2):
            send(piece, piece, es.at[c, d], er.at[c, d], at(dy=d))
        send(piece, piece, fs.at[c, 0], fr.at[c, 0], sibling)

    def rows_core(c):
        for d in (1, 3, 2):
            arrived(C.at[c, :, (x + 4 - d) % 4], cs.at[c, d], cr.at[c, d])
        send(C.at[c, :, :, pl.ds(2 * other, 2)], CS.at[c], gs.at[c], gr.at[c], sibling)
        for d in (1, 3, 2):
            piece = R.at[k, c, (y + 4 - d) % 4]
            arrived(piece, es.at[c, d], er.at[c, d])
            send(piece, piece, fs.at[c, d], fr.at[c, d], sibling)

    def gram_part(c):
        arrived(CS.at[c], gs.at[c], gr.at[c])
        for d in range(4):
            arrived(R.at[other, c, (y + 4 - d) % 4], fs.at[c, d], fr.at[c, d])

        @pl.loop(0, 4)
        def _(f):
            start = pl.multiple_of(f * 256, 256)
            rows = pl.ds(start, 256)
            for half in range(2):
                lanes = slice(half * 256, (half + 1) * 256)
                tile = None if c == 0 else gram[rows, lanes]
                for lane in range(2):
                    left = R[k if lane == 0 else other, c, f].reshape(16 * T, 256)
                    right = C[c, :, :, 2 * k + half] if lane == 0 else CS[c, :, :, half]
                    term = lax.dot_general(
                        left, right.reshape(16 * T, 256), (((0,), (0,)), ((), ())),
                        preferred_element_type=F32,
                    )
                    tile = term if tile is None else tile + term
                if c == PARTS - 1:
                    tile = tile * (2.0 / TOKENS)
                    rid = row * 1024 + start + lax.broadcasted_iota(
                        jnp.int32, (256, 256), 0
                    )
                    cid = col * 512 + half * 256 + lax.broadcasted_iota(
                        jnp.int32, (256, 256), 1
                    )
                    tile = jnp.where(cid >= rid, tile, 0.0)
                gram[rows, lanes] = tile

    steps = {
        "attention_z": attention_z, "attention_y": attention_y, "project": project, "combine": combine,
        "squares": squares, "norm": norm, "multicast": multicast, "rows_z": rows_z,
        "rows_y": rows_y, "rows_core": rows_core, "gram": gram_part,
    }
    order = sorted(
        (start + pitch * c, c, name) for name, start, pitch in STEPS for c in range(PARTS)
    )
    for _, c, name in order:
        steps[name](c)

    arrived(SR, ks.at[3], kr.at[3])
    stream[pl.ds(off_mine, 64), :] = S2[k]
    stream[pl.ds(off_other, 64), :] = SR[...]
    for c, when in sends:
        if when is None:
            c.wait_send()
        else:
            pl.when(when)(c.wait_send)
    for c in range(PARTS):
        for d in range(4):
            yp = (y + 4 - d) % 4
            pl.when(yp != x)(to_x(c, yp).wait_send)
            if d:
                to_zl(c, (zl + d) % 4).wait_send()


def local(attn, w_out, resid, gain):
    dma = pltpu.SemaphoreType.DMA
    vmem = pltpu.VMEM
    whole = pl.BlockSpec(memory_space=pltpu.VMEM)
    anywhere = pl.BlockSpec(memory_space=pl.ANY)
    parts = dma((PARTS, 4))
    return pl.pallas_call(
        kernel,
        out_shape=(
            jax.ShapeDtypeStruct((128, 512), BF16),
            jax.ShapeDtypeStruct((1024, 512), F32),
        ),
        in_specs=[anywhere] * 4,
        out_specs=(whole, whole),
        scratch_shapes=[
            vmem((PARTS, 4, 4, T, 1024), BF16),
            vmem((2, 1024, 512), BF16),
            vmem((PARTS, 4, 4, T, 1024), BF16),
            vmem((PARTS, 4, 4, T, 1024), BF16),
            vmem((PARTS, 4, T, 1024), F32),
            vmem((PARTS, 4, T, 1024), BF16),
            vmem((PARTS, 4, T, 1024), BF16),
            vmem((2, 64, 512), BF16),
            vmem((2, 1, 512), F32),
            vmem((PARTS, T, 1024), F32),
            vmem((2, 64, 512), BF16),
            vmem((64, 512), BF16),
            vmem((PARTS, 1, 128), F32),
            vmem((PARTS, 16, 1, 128), F32),
            vmem((PARTS, 4, T, 256), BF16),
            vmem((PARTS, 4, T, 256), BF16),
            vmem((PARTS, 4, 4, 4, T, 256), BF16),
            vmem((PARTS, 4, 4, 2, T, 256), BF16),
            vmem((2, PARTS, 4, 4, 4, T, 256), BF16),
            dma((3 + PARTS,)), dma((4,)), dma((4,)),
            parts, parts, parts, parts, parts, parts, parts, parts,
            dma((PARTS, 16)), dma((PARTS, 16)),
            parts, parts, parts, parts, parts, parts, parts, parts, parts, parts,
            parts, parts, dma((PARTS,)), dma((PARTS,)), parts,
        ],
        compiler_params=pltpu.CompilerParams(
            collective_id=0, has_side_effects=True, vmem_limit_bytes=60 << 20
        ),
        cost_estimate=pl.CostEstimate(
            flops=4 * 2048 * 1024 * 512, bytes_accessed=16 << 20, transcendentals=128
        ),
    )(attn, w_out, resid, gain.reshape(1, 512))


def solution(mesh):
    placed = (P("col", "row"), P("row", "col"), P("row", "col"), P("col"))
    return jax.shard_map(
        local,
        mesh=mesh,
        in_specs=placed,
        out_specs=(P("row", "col"), P("row", "col")),
        check_vma=False,
    )
```

```python
import jax
import jax.numpy as jnp
from jax import lax
from jax.experimental import pallas as pl
from jax.experimental.pallas import tpu as pltpu
from jax.sharding import PartitionSpec as P

D = 16384
TOKENS = 2048
EPS = 1e-05
MESH = pl.DeviceIdType.MESH
F32 = jnp.float32
BF16 = jnp.bfloat16
PARTS = 4
T = 64 // PARTS
AHEAD = 2
STEPS = (
    ("attention_z", 39, 4), ("attention_y", 43, 4.5), ("project", 51, 5),
    ("combine", 60, 5), ("squares", 65, 5), ("norm", 72, 5), ("rows_z", 77, 5),
    ("rows_y", 82, 5), ("columns_x", 83, 5), ("rows_core", 90, 6), ("gram", 93, 6),
)


def device(x, zl, y, zh, k):
    return (x * 4 + zl, (y * 4 + zh) * 2 + k)


def kernel(
    attn, w_out, resid, gain,
    stream, gram,
    A, W, XS, XR, ACC, ZS, ZR, RB, G, SUM, S2, SR, SQS, SQ, N, C, CS, R,
    loc, ks, kr, zs, zr, ys, yr, xs, xr, ls, lr, qs, qr, hs, hr,
    vs, vr, cs, cr, es, er, fs, fr, gs, gr, us, ur,
):
    row, col = lax.axis_index("row"), lax.axis_index("col")
    x, zl = row // 4, row % 4
    y, zh, k = col // 8, (col // 2) % 4, col % 2
    other = 1 - k

    def at(dx=0, dl=0, dy=0, dh=0):
        return device((x + dx) % 4, (zl + dl) % 4, (y + dy) % 4, (zh + dh) % 4, k)

    sibling = device(x, zl, y, zh, other)
    sends = []

    def copy(src, dst, ssem, rsem, to):
        return pltpu.make_async_remote_copy(
            src_ref=src, dst_ref=dst, send_sem=ssem, recv_sem=rsem,
            device_id=to, device_id_type=MESH,
        )

    def send(src, dst, ssem, rsem, to, when=None):
        c = copy(src, dst, ssem, rsem, to)
        if when is None:
            c.start()
        else:
            pl.when(when)(c.start)
        sends.append((c, when))

    def arrived(dst, ssem, rsem, when=None):
        c = copy(dst, dst, ssem, rsem, sibling)
        if when is None:
            c.wait_recv()
        else:
            pl.when(when)(c.wait_recv)

    off_other = pl.multiple_of(other * 64, 64)
    off_mine = pl.multiple_of(k * 64, 64)
    own = [
        pltpu.make_async_copy(w_out, W.at[k], loc.at[0]),
        pltpu.make_async_copy(resid.at[pl.ds(off_mine, 64)], RB.at[k], loc.at[1]),
        pltpu.make_async_copy(gain, G.at[k], loc.at[2]),
    ] + [
        pltpu.make_async_copy(attn.at[pl.ds(c * T, T)], A.at[c, y, zh], loc.at[3 + c])
        for c in range(PARTS)
    ]
    for c in own:
        c.start()

    bar = pltpu.get_barrier_semaphore()

    def greet(dev, when=None):
        def go():
            pl.semaphore_signal(bar, inc=1, device_id=dev, device_id_type=MESH)
        if when is None:
            go()
        else:
            pl.when(when)(go)

    for dh in (2, 1, 3, 0):
        for dy in (2, 1, 3, 0):
            if dy or dh:
                greet(at(dy=dy, dh=dh))
    diagonal = jnp.logical_and(x == y, zl == zh)
    for sz in range(4):
        for sx in range(4):
            here = jnp.logical_and(sx == x, sz == zl)
            greet(
                device(sx, sz, x, zl, k),
                jnp.logical_not(jnp.logical_and(diagonal, here)),
            )
    greet(sibling)
    for d in range(1, 4):
        greet(at(dx=d))
        greet(at(dl=d))
    pl.semaphore_wait(bar, 22 + 16 - diagonal.astype(jnp.int32))

    def attention_out(c):
        for d in (1, 3):
            send(
                attn.at[pl.ds(c * T, T)], A.at[c, y, zh], zs.at[c, d], zr.at[c, d],
                at(dh=d),
            )

    for c in range(AHEAD):
        attention_out(c)
    send(w_out, W.at[k], ks.at[0], kr.at[0], sibling)
    send(resid.at[pl.ds(off_other, 64)], RB.at[k], ks.at[1], kr.at[1], sibling)
    send(gain, G.at[k], ks.at[2], kr.at[2], sibling)
    for c in own:
        c.wait()
    arrived(W.at[other], ks.at[0], kr.at[0])
    arrived(RB.at[other], ks.at[1], kr.at[1])
    arrived(G.at[other], ks.at[2], kr.at[2])

    def to_x(c, yp):
        return copy(
            XS.at[c, yp], XR.at[c, x], xs.at[c, yp], xr.at[c, x],
            device(yp, zl, y, zh, k),
        )

    def to_zl(c, zp):
        return copy(
            ZS.at[c, zp], ZR.at[c, zl], ls.at[c, zp], lr.at[c, zl],
            device(x, zp, y, zh, k),
        )

    def project_block(c, yp):
        left = A[c, yp].reshape(4 * T, 1024)
        for h in range(2):
            lanes = slice(h * 512, (h + 1) * 512)
            part = jnp.dot(left, W[h], preferred_element_type=F32).reshape(4, T, 512)

            @pl.when(yp == x)
            def _():
                ACC[c, :, :, lanes] = part

            @pl.when(yp != x)
            def _():
                XS[c, yp, :, :, lanes] = part.astype(BF16)

        pl.when(yp != x)(lambda: to_x(c, yp).start())

    def attention_z(c):
        d = 1 if c % 2 == 0 else 3
        piece = A.at[c, y, (zh + 4 - d) % 4]
        arrived(piece, zs.at[c, d], zr.at[c, d])
        send(piece, piece, zs.at[c, 2], zr.at[c, 2], at(dh=d))
        if c + AHEAD < PARTS:
            attention_out(c + AHEAD)

    def attention_y(c):
        for d in ((3, 2) if c % 2 == 0 else (1, 2)):
            arrived(A.at[c, y, (zh + 4 - d) % 4], zs.at[c, d], zr.at[c, d])
        for d in (1, 3, 2):
            send(A.at[c, y], A.at[c, y], ys.at[c, d], yr.at[c, d], at(dy=d))
        project_block(c, y)

    def project(c):
        @pl.loop(1, 4)
        def _(d):
            yp = (y + 4 - d) % 4
            arrived(A.at[c, yp], ys.at[c, d], yr.at[c, d])
            project_block(c, yp)

    def combine(c):
        total = ACC[c]
        for d in range(1, 4):
            src = (x + d) % 4
            arrived(XR.at[c, src], xs.at[c, 0], xr.at[c, src])
            total = total + XR[c, src].astype(F32)
        ACC[c] = total
        ZS[c] = total.astype(BF16)
        for d in (1, 3, 2):
            to_zl(c, (zl + d) % 4).start()

    def squares(c):
        rows = slice(c * T, (c + 1) * T)
        for d in range(1, 4):
            src = (zl + d) % 4
            arrived(ZR.at[c, src], ls.at[c, 0], lr.at[c, src])
        summed_squares = jnp.zeros((T, 1), F32)
        for h in range(2):
            lanes = slice(h * 512, (h + 1) * 512)
            total = ACC[c, zl, :, lanes]
            for d in range(1, 4):
                total = total + ZR[c, (zl + d) % 4, :, lanes].astype(F32)
            total = total + RB[h, rows, :].astype(F32)
            SUM[c, :, lanes] = total
            S2[h, rows, :] = total.astype(BF16)
            summed_squares = summed_squares + jnp.sum(total * total, axis=1, keepdims=True)
        wide = jnp.concatenate(
            [
                jnp.broadcast_to(summed_squares, (T, 128)),
                jnp.zeros((128 - T, 128), F32),
            ],
            axis=0,
        )
        SQS[c] = wide.T[0:1]
        for dh in (2, 1, 3, 0):
            for dy in (2, 1, 3, 0):
                if dy or dh:
                    i = dy * 4 + dh
                    send(
                        SQS.at[c], SQ.at[c, i], qs.at[c, i], qr.at[c, i],
                        at(dy=dy, dh=dh),
                    )
        if c == PARTS - 1:
            send(S2.at[other], SR, ks.at[3], kr.at[3], sibling)

    def norm(c):
        total = SQS[c]
        for i in range(1, 16):
            arrived(SQ.at[c, i], qs.at[c, i], qr.at[c, i])
            total = total + SQ[c, i]
        scale = lax.rsqrt(total / D + EPS)
        scale = jnp.broadcast_to(scale, (128, 128)).T[0:T, 0:1]
        for f in range(4):
            lanes = slice(f * 256, (f + 1) * 256)
            g = G[f // 2, :, (f % 2) * 256:(f % 2) * 256 + 256]
            normed = (SUM[c, :, lanes] * g * scale).astype(BF16)
            N[c, f] = normed
            C[c, zl, x, f] = normed

        up = (zh + (zh < zl).astype(jnp.int32)) % 4
        for i in range(2):
            j = (up + 3 * i) % 4
            for q in range(4):
                away = None
                if i == 0:
                    away = jnp.logical_not(jnp.logical_and(diagonal, q == y))
                send(
                    N.at[c, q], R.at[k, c, q, zl, x],
                    vs.at[c, 4 * i + q], vr.at[c, 4 * zl + x],
                    device(y, zh, q, j, k), away,
                )

        @pl.when(diagonal)
        def _():
            R[k, c, y, zl, x] = N[c, y]

        for d in (1, 3, 2):
            send(N.at[c], C.at[c, zl, x], hs.at[c, d], hr.at[c, d], at(dl=d))

    def columns_x(c):
        for d in (1, 3, 2):
            arrived(C.at[c, (zl + 4 - d) % 4, x], hs.at[c, d], hr.at[c, d])
        for d in (1, 3, 2):
            piece = C.at[c, :, x]
            send(piece, piece, cs.at[c, d], cr.at[c, d], at(dx=d))

    def direct(sz):
        up = (zl + (zl < sz).astype(jnp.int32)) % 4
        return zh == up, zh == (up + 3) % 4

    def rows_z(c):
        for sz in range(4):
            below, above = direct(sz)
            first = jnp.logical_or(below, above)
            for sx in range(4):
                here = jnp.logical_and(sx == x, sz == zl)
                arrived(
                    R.at[k, c, y, sz, sx], vs.at[c, 0], vr.at[c, 4 * sz + sx],
                    jnp.logical_and(
                        first, jnp.logical_not(jnp.logical_and(diagonal, here))
                    ),
                )
            piece = R.at[k, c, y, sz]
            to = jnp.where(below, 1, 3)
            send(piece, piece, us.at[c, sz], ur.at[c, sz], at(dh=to), first)

    def rows_y(c):
        piece = R.at[k, c, y]
        for sz in range(4):
            below, above = direct(sz)
            arrived(
                R.at[k, c, y, sz], us.at[c, sz], ur.at[c, sz],
                jnp.logical_not(jnp.logical_or(below, above)),
            )
        for d in (1, 3, 2):
            send(piece, piece, es.at[c, d], er.at[c, d], at(dy=d))
        send(piece, piece, fs.at[c, 0], fr.at[c, 0], sibling)

    def rows_core(c):
        for d in (1, 3, 2):
            arrived(C.at[c, :, (x + 4 - d) % 4], cs.at[c, d], cr.at[c, d])
        send(C.at[c, :, :, pl.ds(2 * other, 2)], CS.at[c], gs.at[c], gr.at[c], sibling)
        for d in (1, 3, 2):
            piece = R.at[k, c, (y + 4 - d) % 4]
            arrived(piece, es.at[c, d], er.at[c, d])
            send(piece, piece, fs.at[c, d], fr.at[c, d], sibling)

    def gram_part(c):
        arrived(CS.at[c], gs.at[c], gr.at[c])
        for d in range(4):
            arrived(R.at[other, c, (y + 4 - d) % 4], fs.at[c, d], fr.at[c, d])

        @pl.loop(0, 4)
        def _(f):
            start = pl.multiple_of(f * 256, 256)
            rows = pl.ds(start, 256)
            for half in range(2):
                lanes = slice(half * 256, (half + 1) * 256)
                tile = None if c == 0 else gram[rows, lanes]
                for lane in range(2):
                    left = R[k if lane == 0 else other, c, f].reshape(16 * T, 256)
                    right = C[c, :, :, 2 * k + half] if lane == 0 else CS[c, :, :, half]
                    term = lax.dot_general(
                        left, right.reshape(16 * T, 256), (((0,), (0,)), ((), ())),
                        preferred_element_type=F32,
                    )
                    tile = term if tile is None else tile + term
                if c == PARTS - 1:
                    tile = tile * (2.0 / TOKENS)
                    rid = row * 1024 + start + lax.broadcasted_iota(
                        jnp.int32, (256, 256), 0
                    )
                    cid = col * 512 + half * 256 + lax.broadcasted_iota(
                        jnp.int32, (256, 256), 1
                    )
                    tile = jnp.where(cid >= rid, tile, 0.0)
                gram[rows, lanes] = tile

    steps = {
        "attention_z": attention_z, "attention_y": attention_y, "project": project, "combine": combine,
        "squares": squares, "norm": norm, "columns_x": columns_x, "rows_z": rows_z,
        "rows_y": rows_y, "rows_core": rows_core, "gram": gram_part,
    }
    order = sorted(
        (start + pitch * c, c, name) for name, start, pitch in STEPS for c in range(PARTS)
    )
    for _, c, name in order:
        steps[name](c)

    arrived(SR, ks.at[3], kr.at[3])
    stream[pl.ds(off_mine, 64), :] = S2[k]
    stream[pl.ds(off_other, 64), :] = SR[...]
    for c, when in sends:
        if when is None:
            c.wait_send()
        else:
            pl.when(when)(c.wait_send)
    for c in range(PARTS):
        for d in range(4):
            yp = (y + 4 - d) % 4
            pl.when(yp != x)(to_x(c, yp).wait_send)
            if d:
                to_zl(c, (zl + d) % 4).wait_send()


def local(attn, w_out, resid, gain):
    dma = pltpu.SemaphoreType.DMA
    vmem = pltpu.VMEM
    whole = pl.BlockSpec(memory_space=pltpu.VMEM)
    anywhere = pl.BlockSpec(memory_space=pl.ANY)
    parts, sixteen = dma((PARTS, 4)), dma((PARTS, 16))
    return pl.pallas_call(
        kernel,
        out_shape=(
            jax.ShapeDtypeStruct((128, 512), BF16),
            jax.ShapeDtypeStruct((1024, 512), F32),
        ),
        in_specs=[anywhere] * 4,
        out_specs=(whole, whole),
        scratch_shapes=[
            vmem((PARTS, 4, 4, T, 1024), BF16),
            vmem((2, 1024, 512), BF16),
            vmem((PARTS, 4, 4, T, 1024), BF16),
            vmem((PARTS, 4, 4, T, 1024), BF16),
            vmem((PARTS, 4, T, 1024), F32),
            vmem((PARTS, 4, T, 1024), BF16),
            vmem((PARTS, 4, T, 1024), BF16),
            vmem((2, 64, 512), BF16),
            vmem((2, 1, 512), F32),
            vmem((PARTS, T, 1024), F32),
            vmem((2, 64, 512), BF16),
            vmem((64, 512), BF16),
            vmem((PARTS, 1, 128), F32),
            vmem((PARTS, 16, 1, 128), F32),
            vmem((PARTS, 4, T, 256), BF16),
            vmem((PARTS, 4, 4, 4, T, 256), BF16),
            vmem((PARTS, 4, 4, 2, T, 256), BF16),
            vmem((2, PARTS, 4, 4, 4, T, 256), BF16),
            dma((3 + PARTS,)), dma((4,)), dma((4,)),
            parts, parts, parts, parts, parts, parts, parts, parts,
            sixteen, sixteen, parts, parts, sixteen, sixteen,
            parts, parts, parts, parts, parts, parts,
            dma((PARTS,)), dma((PARTS,)), parts, parts,
        ],
        compiler_params=pltpu.CompilerParams(
            collective_id=0, has_side_effects=True, vmem_limit_bytes=40 << 20
        ),
        cost_estimate=pl.CostEstimate(
            flops=4 * 2048 * 1024 * 512, bytes_accessed=16 << 20, transcendentals=128
        ),
    )(attn, w_out, resid, gain.reshape(1, 512))


def solution(mesh):
    placed = (P("col", "row"), P("row", "col"), P("row", "col"), P("col"))
    return jax.shard_map(
        local,
        mesh=mesh,
        in_specs=placed,
        out_specs=(P("row", "col"), P("row", "col")),
        check_vma=False,
    )
```

```python
import jax
import jax.numpy as jnp
from jax import lax
from jax.experimental import pallas as pl
from jax.experimental.pallas import tpu as pltpu
from jax.sharding import PartitionSpec as P

D = 16384
TOKENS = 2048
EPS = 1e-05
MESH = pl.DeviceIdType.MESH
F32 = jnp.float32
BF16 = jnp.bfloat16
PARTS = 4
T = 64 // PARTS
AHEAD = 2
DIRECT = 1
STEPS = (
    ("attention_z", 39, 4), ("attention_y", 43, 4.5), ("project", 51, 5),
    ("combine", 60, 5), ("squares", 65, 5), ("norm", 72, 5), ("rows_z", 77, 5),
    ("rows_y", 82, 5), ("columns_x", 83, 5), ("rows_core", 90, 6), ("gram", 93, 6),
)


def device(x, zl, y, zh, k):
    return (x * 4 + zl, (y * 4 + zh) * 2 + k)


def kernel(
    attn, w_out, resid, gain,
    stream, gram,
    A, W, XS, XR, ACC, ZS, ZR, RB, G, SUM, S2, SR, SQS, SQ, N, C, CS, R,
    loc, ks, kr, zs, zr, ys, yr, xs, xr, ls, lr, qs, qr, hs, hr,
    vs, vr, cs, cr, es, er, fs, fr, gs, gr, us, ur,
):
    row, col = lax.axis_index("row"), lax.axis_index("col")
    x, zl = row // 4, row % 4
    y, zh, k = col // 8, (col // 2) % 4, col % 2
    other = 1 - k

    def at(dx=0, dl=0, dy=0, dh=0):
        return device((x + dx) % 4, (zl + dl) % 4, (y + dy) % 4, (zh + dh) % 4, k)

    sibling = device(x, zl, y, zh, other)
    sends = []

    def copy(src, dst, ssem, rsem, to):
        return pltpu.make_async_remote_copy(
            src_ref=src, dst_ref=dst, send_sem=ssem, recv_sem=rsem,
            device_id=to, device_id_type=MESH,
        )

    def send(src, dst, ssem, rsem, to, when=None):
        c = copy(src, dst, ssem, rsem, to)
        if when is None:
            c.start()
        else:
            pl.when(when)(c.start)
        sends.append((c, when))

    def arrived(dst, ssem, rsem, when=None):
        c = copy(dst, dst, ssem, rsem, sibling)
        if when is None:
            c.wait_recv()
        else:
            pl.when(when)(c.wait_recv)

    off_other = pl.multiple_of(other * 64, 64)
    off_mine = pl.multiple_of(k * 64, 64)
    own = [
        pltpu.make_async_copy(w_out, W.at[k], loc.at[0]),
        pltpu.make_async_copy(resid.at[pl.ds(off_mine, 64)], RB.at[k], loc.at[1]),
        pltpu.make_async_copy(gain, G.at[k], loc.at[2]),
    ] + [
        pltpu.make_async_copy(attn.at[pl.ds(c * T, T)], A.at[c, y, zh], loc.at[3 + c])
        for c in range(PARTS)
    ]
    for c in own:
        c.start()

    bar = pltpu.get_barrier_semaphore()

    def greet(dev, when=None):
        def go():
            pl.semaphore_signal(bar, inc=1, device_id=dev, device_id_type=MESH)
        if when is None:
            go()
        else:
            pl.when(when)(go)

    for dh in (2, 1, 3, 0):
        for dy in (2, 1, 3, 0):
            if dy or dh:
                greet(at(dy=dy, dh=dh))
    diagonal = jnp.logical_and(x == y, zl == zh)
    for sz in range(4):
        for sx in range(4):
            here = jnp.logical_and(sx == x, sz == zl)
            greet(
                device(sx, sz, x, zl, k),
                jnp.logical_not(jnp.logical_and(diagonal, here)),
            )
    greet(sibling)
    for d in range(1, 4):
        greet(at(dx=d))
        greet(at(dl=d))
    pl.semaphore_wait(bar, 22 + 16 - diagonal.astype(jnp.int32))

    def attention_out(c):
        for d in (1, 3) if c >= DIRECT else (1, 3, 2):
            send(
                attn.at[pl.ds(c * T, T)], A.at[c, y, zh], zs.at[c, d], zr.at[c, d],
                at(dh=d),
            )

    for c in range(AHEAD):
        attention_out(c)
    send(w_out, W.at[k], ks.at[0], kr.at[0], sibling)
    send(resid.at[pl.ds(off_other, 64)], RB.at[k], ks.at[1], kr.at[1], sibling)
    send(gain, G.at[k], ks.at[2], kr.at[2], sibling)
    for c in own:
        c.wait()
    arrived(W.at[other], ks.at[0], kr.at[0])
    arrived(RB.at[other], ks.at[1], kr.at[1])
    arrived(G.at[other], ks.at[2], kr.at[2])

    def nearest(i):
        return i + i // 2 - 2 * (i // 3)

    def to_x(c, yp):
        return copy(
            XS.at[c, yp], XR.at[c, x], xs.at[c, yp], xr.at[c, x],
            device(yp, zl, y, zh, k),
        )

    def to_zl(c, zp):
        return copy(
            ZS.at[c, zp], ZR.at[c, zl], ls.at[c, zp], lr.at[c, zl],
            device(x, zp, y, zh, k),
        )

    def project_block(c, yp):
        left = A[c, yp].reshape(4 * T, 1024)
        for h in range(2):
            lanes = slice(h * 512, (h + 1) * 512)
            part = jnp.dot(left, W[h], preferred_element_type=F32).reshape(4, T, 512)

            @pl.when(yp == x)
            def _():
                ACC[c, :, :, lanes] = part

            @pl.when(yp != x)
            def _():
                XS[c, yp, :, :, lanes] = part.astype(BF16)

        pl.when(yp != x)(lambda: to_x(c, yp).start())

    def attention_z(c):
        d = 1 if c % 2 == 0 else 3
        piece = A.at[c, y, (zh + 4 - d) % 4]
        arrived(piece, zs.at[c, d], zr.at[c, d])
        if c >= DIRECT:
            send(piece, piece, zs.at[c, 2], zr.at[c, 2], at(dh=d))
        if c + AHEAD < PARTS:
            attention_out(c + AHEAD)

    def attention_y(c):
        for d in ((3, 2) if c % 2 == 0 else (1, 2)):
            arrived(A.at[c, y, (zh + 4 - d) % 4], zs.at[c, d], zr.at[c, d])
        for d in (1, 3, 2):
            send(A.at[c, y], A.at[c, y], ys.at[c, d], yr.at[c, d], at(dy=d))
        project_block(c, y)

    def project(c):
        @pl.loop(1, 4)
        def _(i):
            d = nearest(i)
            yp = (y + 4 - d) % 4
            arrived(A.at[c, yp], ys.at[c, d], yr.at[c, d])
            project_block(c, yp)

    def combine(c):
        total = ACC[c]
        for d in range(1, 4):
            src = (x + d) % 4
            arrived(XR.at[c, src], xs.at[c, 0], xr.at[c, src])
            total = total + XR[c, src].astype(F32)
        ACC[c] = total
        ZS[c] = total.astype(BF16)
        for d in (1, 3, 2):
            to_zl(c, (zl + d) % 4).start()

    def squares(c):
        rows = slice(c * T, (c + 1) * T)
        for d in range(1, 4):
            src = (zl + d) % 4
            arrived(ZR.at[c, src], ls.at[c, 0], lr.at[c, src])
        summed_squares = jnp.zeros((T, 1), F32)
        for h in range(2):
            lanes = slice(h * 512, (h + 1) * 512)
            total = ACC[c, zl, :, lanes]
            for d in range(1, 4):
                total = total + ZR[c, (zl + d) % 4, :, lanes].astype(F32)
            total = total + RB[h, rows, :].astype(F32)
            SUM[c, :, lanes] = total
            S2[h, rows, :] = total.astype(BF16)
            summed_squares = summed_squares + jnp.sum(total * total, axis=1, keepdims=True)
        wide = jnp.concatenate(
            [
                jnp.broadcast_to(summed_squares, (T, 128)),
                jnp.zeros((128 - T, 128), F32),
            ],
            axis=0,
        )
        SQS[c] = wide.T[0:1]
        for dh in (2, 1, 3, 0):
            for dy in (2, 1, 3, 0):
                if dy or dh:
                    i = dy * 4 + dh
                    send(
                        SQS.at[c], SQ.at[c, i], qs.at[c, i], qr.at[c, i],
                        at(dy=dy, dh=dh),
                    )
        if c == PARTS - 1:
            send(S2.at[other], SR, ks.at[3], kr.at[3], sibling)

    def norm(c):
        total = SQS[c]
        for i in range(1, 16):
            arrived(SQ.at[c, i], qs.at[c, i], qr.at[c, i])
            total = total + SQ[c, i]
        scale = lax.rsqrt(total / D + EPS)
        scale = jnp.broadcast_to(scale, (128, 128)).T[0:T, 0:1]
        for f in range(4):
            lanes = slice(f * 256, (f + 1) * 256)
            g = G[f // 2, :, (f % 2) * 256:(f % 2) * 256 + 256]
            normed = (SUM[c, :, lanes] * g * scale).astype(BF16)
            N[c, f] = normed
            C[c, zl, x, f] = normed

        up = (zh + (zh < zl).astype(jnp.int32)) % 4
        for i in range(2):
            j = (up + 3 * i) % 4
            for q in range(4):
                away = None
                if i == 0:
                    away = jnp.logical_not(jnp.logical_and(diagonal, q == y))
                send(
                    N.at[c, q], R.at[k, c, q, zl, x],
                    vs.at[c, 4 * i + q], vr.at[c, 4 * zl + x],
                    device(y, zh, q, j, k), away,
                )

        @pl.when(diagonal)
        def _():
            R[k, c, y, zl, x] = N[c, y]

        for d in (1, 3, 2):
            send(N.at[c], C.at[c, zl, x], hs.at[c, d], hr.at[c, d], at(dl=d))

    def columns_x(c):
        for d in (1, 3, 2):
            arrived(C.at[c, (zl + 4 - d) % 4, x], hs.at[c, d], hr.at[c, d])
        for d in (1, 3, 2):
            piece = C.at[c, :, x]
            send(piece, piece, cs.at[c, d], cr.at[c, d], at(dx=d))

    def direct(sz):
        up = (zl + (zl < sz).astype(jnp.int32)) % 4
        return zh == up, zh == (up + 3) % 4

    def rows_z(c):
        for sz in range(4):
            below, above = direct(sz)
            first = jnp.logical_or(below, above)
            for sx in range(4):
                here = jnp.logical_and(sx == x, sz == zl)
                arrived(
                    R.at[k, c, y, sz, sx], vs.at[c, 0], vr.at[c, 4 * sz + sx],
                    jnp.logical_and(
                        first, jnp.logical_not(jnp.logical_and(diagonal, here))
                    ),
                )
            piece = R.at[k, c, y, sz]
            to = jnp.where(below, 1, 3)
            send(piece, piece, us.at[c, sz], ur.at[c, sz], at(dh=to), first)

    def rows_y(c):
        piece = R.at[k, c, y]
        for sz in range(4):
            below, above = direct(sz)
            arrived(
                R.at[k, c, y, sz], us.at[c, sz], ur.at[c, sz],
                jnp.logical_not(jnp.logical_or(below, above)),
            )
        for d in (1, 3, 2):
            send(piece, piece, es.at[c, d], er.at[c, d], at(dy=d))
        send(piece, piece, fs.at[c, 0], fr.at[c, 0], sibling)

    def rows_core(c):
        for d in (1, 3, 2):
            arrived(C.at[c, :, (x + 4 - d) % 4], cs.at[c, d], cr.at[c, d])
        send(C.at[c, :, :, pl.ds(2 * other, 2)], CS.at[c], gs.at[c], gr.at[c], sibling)
        for d in (1, 3, 2):
            piece = R.at[k, c, (y + 4 - d) % 4]
            arrived(piece, es.at[c, d], er.at[c, d])
            send(piece, piece, fs.at[c, d], fr.at[c, d], sibling)

    def gram_part(c):
        arrived(CS.at[c], gs.at[c], gr.at[c])

        @pl.loop(0, 4)
        def _(i):
            d = nearest(i)
            f = (y + 4 - d) % 4
            arrived(R.at[other, c, f], fs.at[c, d], fr.at[c, d])
            start = pl.multiple_of(f * 256, 256)
            rows = pl.ds(start, 256)
            for half in range(2):
                lanes = slice(half * 256, (half + 1) * 256)
                tile = None if c == 0 else gram[rows, lanes]
                for lane in range(2):
                    left = R[k if lane == 0 else other, c, f].reshape(16 * T, 256)
                    right = C[c, :, :, 2 * k + half] if lane == 0 else CS[c, :, :, half]
                    term = lax.dot_general(
                        left, right.reshape(16 * T, 256), (((0,), (0,)), ((), ())),
                        preferred_element_type=F32,
                    )
                    tile = term if tile is None else tile + term
                if c == PARTS - 1:
                    tile = tile * (2.0 / TOKENS)
                    rid = row * 1024 + start + lax.broadcasted_iota(
                        jnp.int32, (256, 256), 0
                    )
                    cid = col * 512 + half * 256 + lax.broadcasted_iota(
                        jnp.int32, (256, 256), 1
                    )
                    tile = jnp.where(cid >= rid, tile, 0.0)
                gram[rows, lanes] = tile

    steps = {
        "attention_z": attention_z, "attention_y": attention_y, "project": project, "combine": combine,
        "squares": squares, "norm": norm, "columns_x": columns_x, "rows_z": rows_z,
        "rows_y": rows_y, "rows_core": rows_core, "gram": gram_part,
    }
    order = sorted(
        (start + pitch * c, c, name) for name, start, pitch in STEPS for c in range(PARTS)
    )
    for _, c, name in order:
        steps[name](c)

    arrived(SR, ks.at[3], kr.at[3])
    stream[pl.ds(off_mine, 64), :] = S2[k]
    stream[pl.ds(off_other, 64), :] = SR[...]
    for c, when in sends:
        if when is None:
            c.wait_send()
        else:
            pl.when(when)(c.wait_send)
    for c in range(PARTS):
        for d in range(4):
            yp = (y + 4 - d) % 4
            pl.when(yp != x)(to_x(c, yp).wait_send)
            if d:
                to_zl(c, (zl + d) % 4).wait_send()


def local(attn, w_out, resid, gain):
    dma = pltpu.SemaphoreType.DMA
    vmem = pltpu.VMEM
    whole = pl.BlockSpec(memory_space=pltpu.VMEM)
    anywhere = pl.BlockSpec(memory_space=pl.ANY)
    parts, sixteen = dma((PARTS, 4)), dma((PARTS, 16))
    return pl.pallas_call(
        kernel,
        out_shape=(
            jax.ShapeDtypeStruct((128, 512), BF16),
            jax.ShapeDtypeStruct((1024, 512), F32),
        ),
        in_specs=[anywhere] * 4,
        out_specs=(whole, whole),
        scratch_shapes=[
            vmem((PARTS, 4, 4, T, 1024), BF16),
            vmem((2, 1024, 512), BF16),
            vmem((PARTS, 4, 4, T, 1024), BF16),
            vmem((PARTS, 4, 4, T, 1024), BF16),
            vmem((PARTS, 4, T, 1024), F32),
            vmem((PARTS, 4, T, 1024), BF16),
            vmem((PARTS, 4, T, 1024), BF16),
            vmem((2, 64, 512), BF16),
            vmem((2, 1, 512), F32),
            vmem((PARTS, T, 1024), F32),
            vmem((2, 64, 512), BF16),
            vmem((64, 512), BF16),
            vmem((PARTS, 1, 128), F32),
            vmem((PARTS, 16, 1, 128), F32),
            vmem((PARTS, 4, T, 256), BF16),
            vmem((PARTS, 4, 4, 4, T, 256), BF16),
            vmem((PARTS, 4, 4, 2, T, 256), BF16),
            vmem((2, PARTS, 4, 4, 4, T, 256), BF16),
            dma((3 + PARTS,)), dma((4,)), dma((4,)),
            parts, parts, parts, parts, parts, parts, parts, parts,
            sixteen, sixteen, parts, parts, sixteen, sixteen,
            parts, parts, parts, parts, parts, parts,
            dma((PARTS,)), dma((PARTS,)), parts, parts,
        ],
        compiler_params=pltpu.CompilerParams(
            collective_id=0, has_side_effects=True, vmem_limit_bytes=40 << 20
        ),
        cost_estimate=pl.CostEstimate(
            flops=4 * 2048 * 1024 * 512, bytes_accessed=16 << 20, transcendentals=128
        ),
    )(attn, w_out, resid, gain.reshape(1, 512))


def solution(mesh):
    placed = (P("col", "row"), P("row", "col"), P("row", "col"), P("col"))
    return jax.shard_map(
        local,
        mesh=mesh,
        in_specs=placed,
        out_specs=(P("row", "col"), P("row", "col")),
        check_vma=False,
    )
```

```python
import jax
import jax.numpy as jnp
from jax import lax
from jax.experimental import pallas as pl
from jax.experimental.pallas import tpu as pltpu
from jax.sharding import PartitionSpec as P

D = 16384
TOKENS = 2048
EPS = 1e-05
MESH = pl.DeviceIdType.MESH
F32 = jnp.float32
BF16 = jnp.bfloat16
PARTS = 4
T = 64 // PARTS
AHEAD = 2
DIRECT = 2
STEPS = (
    ("attention_z", 39, 4), ("attention_y", 43, 4.5), ("project", 51, 5),
    ("combine", 60, 5), ("squares", 65, 5), ("norm", 72, 5), ("rows_z", 77, 5),
    ("rows_y", 82, 5), ("columns_x", 83, 5), ("rows_core", 90, 6), ("gram", 93, 6),
)


def device(x, zl, y, zh, k):
    return (x * 4 + zl, (y * 4 + zh) * 2 + k)


def kernel(
    attn, w_out, resid, gain,
    stream, gram,
    A, W, XS, XR, ACC, ZS, ZR, RB, G, SUM, S2, SR, SQS, SQ, N, C, CS, R,
    loc, ks, kr, zs, zr, ys, yr, xs, xr, ls, lr, qs, qr, hs, hr,
    vs, vr, cs, cr, es, er, fs, fr, gs, gr, us, ur,
):
    row, col = lax.axis_index("row"), lax.axis_index("col")
    x, zl = row // 4, row % 4
    y, zh, k = col // 8, (col // 2) % 4, col % 2
    other = 1 - k

    def at(dx=0, dl=0, dy=0, dh=0):
        return device((x + dx) % 4, (zl + dl) % 4, (y + dy) % 4, (zh + dh) % 4, k)

    sibling = device(x, zl, y, zh, other)
    sends = []

    def copy(src, dst, ssem, rsem, to):
        return pltpu.make_async_remote_copy(
            src_ref=src, dst_ref=dst, send_sem=ssem, recv_sem=rsem,
            device_id=to, device_id_type=MESH,
        )

    def send(src, dst, ssem, rsem, to, when=None):
        c = copy(src, dst, ssem, rsem, to)
        if when is None:
            c.start()
        else:
            pl.when(when)(c.start)
        sends.append((c, when))

    def arrived(dst, ssem, rsem, when=None):
        c = copy(dst, dst, ssem, rsem, sibling)
        if when is None:
            c.wait_recv()
        else:
            pl.when(when)(c.wait_recv)

    off_other = pl.multiple_of(other * 64, 64)
    off_mine = pl.multiple_of(k * 64, 64)
    own = [
        pltpu.make_async_copy(w_out, W.at[k], loc.at[0]),
        pltpu.make_async_copy(resid.at[pl.ds(off_mine, 64)], RB.at[k], loc.at[1]),
        pltpu.make_async_copy(gain, G.at[k], loc.at[2]),
    ] + [
        pltpu.make_async_copy(attn.at[pl.ds(c * T, T)], A.at[c, y, zh], loc.at[3 + c])
        for c in range(PARTS)
    ]
    for c in own:
        c.start()

    bar = pltpu.get_barrier_semaphore()

    def greet(dev, when=None):
        def go():
            pl.semaphore_signal(bar, inc=1, device_id=dev, device_id_type=MESH)
        if when is None:
            go()
        else:
            pl.when(when)(go)

    for dh in (2, 1, 3, 0):
        for dy in (2, 1, 3, 0):
            if dy or dh:
                greet(at(dy=dy, dh=dh))
    diagonal = jnp.logical_and(x == y, zl == zh)
    for sz in range(4):
        for sx in range(4):
            here = jnp.logical_and(sx == x, sz == zl)
            greet(
                device(sx, sz, x, zl, k),
                jnp.logical_not(jnp.logical_and(diagonal, here)),
            )
    greet(sibling)
    for d in range(1, 4):
        greet(at(dx=d))
        greet(at(dl=d))
    pl.semaphore_wait(bar, 22 + 16 - diagonal.astype(jnp.int32))

    def attention_out(c):
        for d in (1, 3) if c >= DIRECT else (1, 3, 2):
            send(
                attn.at[pl.ds(c * T, T)], A.at[c, y, zh], zs.at[c, d], zr.at[c, d],
                at(dh=d),
            )

    for c in range(AHEAD):
        attention_out(c)
    send(w_out, W.at[k], ks.at[0], kr.at[0], sibling)
    send(resid.at[pl.ds(off_other, 64)], RB.at[k], ks.at[1], kr.at[1], sibling)
    send(gain, G.at[k], ks.at[2], kr.at[2], sibling)
    for c in own:
        c.wait()
    arrived(W.at[other], ks.at[0], kr.at[0])
    arrived(RB.at[other], ks.at[1], kr.at[1])
    arrived(G.at[other], ks.at[2], kr.at[2])

    def nearest(i):
        return i + i // 2 - 2 * (i // 3)

    def to_x(c, yp):
        return copy(
            XS.at[c, yp], XR.at[c, x], xs.at[c, yp], xr.at[c, x],
            device(yp, zl, y, zh, k),
        )

    def to_zl(c, zp):
        return copy(
            ZS.at[c, zp], ZR.at[c, zl], ls.at[c, zp], lr.at[c, zl],
            device(x, zp, y, zh, k),
        )

    def project_block(c, yp):
        left = A[c, yp].reshape(4 * T, 1024)
        for h in range(2):
            lanes = slice(h * 512, (h + 1) * 512)
            part = jnp.dot(left, W[h], preferred_element_type=F32).reshape(4, T, 512)

            @pl.when(yp == x)
            def _():
                ACC[c, :, :, lanes] = part

            @pl.when(yp != x)
            def _():
                XS[c, yp, :, :, lanes] = part.astype(BF16)

        pl.when(yp != x)(lambda: to_x(c, yp).start())

    def attention_z(c):
        d = 1 if c % 2 == 0 else 3
        piece = A.at[c, y, (zh + 4 - d) % 4]
        arrived(piece, zs.at[c, d], zr.at[c, d])
        if c >= DIRECT:
            send(piece, piece, zs.at[c, 2], zr.at[c, 2], at(dh=d))
        if c + AHEAD < PARTS:
            attention_out(c + AHEAD)

    def attention_y(c):
        for d in ((3, 2) if c % 2 == 0 else (1, 2)):
            arrived(A.at[c, y, (zh + 4 - d) % 4], zs.at[c, d], zr.at[c, d])
        for d in (1, 3, 2):
            send(A.at[c, y], A.at[c, y], ys.at[c, d], yr.at[c, d], at(dy=d))
        project_block(c, y)

    def project(c):
        @pl.loop(1, 4)
        def _(i):
            d = nearest(i)
            yp = (y + 4 - d) % 4
            arrived(A.at[c, yp], ys.at[c, d], yr.at[c, d])
            project_block(c, yp)

    def combine(c):
        total = ACC[c]
        for d in range(1, 4):
            src = (x + d) % 4
            arrived(XR.at[c, src], xs.at[c, 0], xr.at[c, src])
            total = total + XR[c, src].astype(F32)
        ACC[c] = total
        ZS[c] = total.astype(BF16)
        for d in (1, 3, 2):
            to_zl(c, (zl + d) % 4).start()

    def squares(c):
        rows = slice(c * T, (c + 1) * T)
        for d in range(1, 4):
            src = (zl + d) % 4
            arrived(ZR.at[c, src], ls.at[c, 0], lr.at[c, src])
        summed_squares = jnp.zeros((T, 1), F32)
        for h in range(2):
            lanes = slice(h * 512, (h + 1) * 512)
            total = ACC[c, zl, :, lanes]
            for d in range(1, 4):
                total = total + ZR[c, (zl + d) % 4, :, lanes].astype(F32)
            total = total + RB[h, rows, :].astype(F32)
            SUM[c, :, lanes] = total
            S2[h, rows, :] = total.astype(BF16)
            summed_squares = summed_squares + jnp.sum(total * total, axis=1, keepdims=True)
        wide = jnp.concatenate(
            [
                jnp.broadcast_to(summed_squares, (T, 128)),
                jnp.zeros((128 - T, 128), F32),
            ],
            axis=0,
        )
        SQS[c] = wide.T[0:1]
        for dh in (2, 1, 3, 0):
            for dy in (2, 1, 3, 0):
                if dy or dh:
                    i = dy * 4 + dh
                    send(
                        SQS.at[c], SQ.at[c, i], qs.at[c, i], qr.at[c, i],
                        at(dy=dy, dh=dh),
                    )
        if c == PARTS - 1:
            send(S2.at[other], SR, ks.at[3], kr.at[3], sibling)

    def norm(c):
        total = SQS[c]
        for i in range(1, 16):
            arrived(SQ.at[c, i], qs.at[c, i], qr.at[c, i])
            total = total + SQ[c, i]
        scale = lax.rsqrt(total / D + EPS)
        scale = jnp.broadcast_to(scale, (128, 128)).T[0:T, 0:1]
        for f in range(4):
            lanes = slice(f * 256, (f + 1) * 256)
            g = G[f // 2, :, (f % 2) * 256:(f % 2) * 256 + 256]
            normed = (SUM[c, :, lanes] * g * scale).astype(BF16)
            N[c, f] = normed
            C[c, zl, x, f] = normed

        up = (zh + (zh < zl).astype(jnp.int32)) % 4
        for i in range(2):
            j = (up + 3 * i) % 4
            for q in range(4):
                away = None
                if i == 0:
                    away = jnp.logical_not(jnp.logical_and(diagonal, q == y))
                send(
                    N.at[c, q], R.at[k, c, q, zl, x],
                    vs.at[c, 4 * i + q], vr.at[c, 4 * zl + x],
                    device(y, zh, q, j, k), away,
                )

        @pl.when(diagonal)
        def _():
            R[k, c, y, zl, x] = N[c, y]

        for d in (1, 3, 2):
            send(N.at[c], C.at[c, zl, x], hs.at[c, d], hr.at[c, d], at(dl=d))

    def columns_x(c):
        for d in (1, 3, 2):
            arrived(C.at[c, (zl + 4 - d) % 4, x], hs.at[c, d], hr.at[c, d])
        for d in (1, 3, 2):
            piece = C.at[c, :, x]
            send(piece, piece, cs.at[c, d], cr.at[c, d], at(dx=d))

    def direct(sz):
        up = (zl + (zl < sz).astype(jnp.int32)) % 4
        return zh == up, zh == (up + 3) % 4

    def rows_z(c):
        for sz in range(4):
            below, above = direct(sz)
            first = jnp.logical_or(below, above)
            for sx in range(4):
                here = jnp.logical_and(sx == x, sz == zl)
                arrived(
                    R.at[k, c, y, sz, sx], vs.at[c, 0], vr.at[c, 4 * sz + sx],
                    jnp.logical_and(
                        first, jnp.logical_not(jnp.logical_and(diagonal, here))
                    ),
                )
            piece = R.at[k, c, y, sz]
            to = jnp.where(below, 1, 3)
            send(piece, piece, us.at[c, sz], ur.at[c, sz], at(dh=to), first)

    def rows_y(c):
        piece = R.at[k, c, y]
        for sz in range(4):
            below, above = direct(sz)
            arrived(
                R.at[k, c, y, sz], us.at[c, sz], ur.at[c, sz],
                jnp.logical_not(jnp.logical_or(below, above)),
            )
        for d in (1, 3, 2):
            send(piece, piece, es.at[c, d], er.at[c, d], at(dy=d))
        send(piece, piece, fs.at[c, 0], fr.at[c, 0], sibling)

    def rows_core(c):
        for d in (1, 3, 2):
            arrived(C.at[c, :, (x + 4 - d) % 4], cs.at[c, d], cr.at[c, d])
        send(C.at[c, :, :, pl.ds(2 * other, 2)], CS.at[c], gs.at[c], gr.at[c], sibling)
        for d in (1, 3, 2):
            piece = R.at[k, c, (y + 4 - d) % 4]
            arrived(piece, es.at[c, d], er.at[c, d])
            send(piece, piece, fs.at[c, d], fr.at[c, d], sibling)

    def gram_part(c):
        arrived(CS.at[c], gs.at[c], gr.at[c])

        @pl.loop(0, 4)
        def _(i):
            d = nearest(i)
            f = (y + 4 - d) % 4
            arrived(R.at[other, c, f], fs.at[c, d], fr.at[c, d])
            start = pl.multiple_of(f * 256, 256)
            rows = pl.ds(start, 256)
            for half in range(2):
                lanes = slice(half * 256, (half + 1) * 256)
                tile = None if c == 0 else gram[rows, lanes]
                for lane in range(2):
                    left = R[k if lane == 0 else other, c, f].reshape(16 * T, 256)
                    right = C[c, :, :, 2 * k + half] if lane == 0 else CS[c, :, :, half]
                    term = lax.dot_general(
                        left, right.reshape(16 * T, 256), (((0,), (0,)), ((), ())),
                        preferred_element_type=F32,
                    )
                    tile = term if tile is None else tile + term
                if c == PARTS - 1:
                    tile = tile * (2.0 / TOKENS)
                    rid = row * 1024 + start + lax.broadcasted_iota(
                        jnp.int32, (256, 256), 0
                    )
                    cid = col * 512 + half * 256 + lax.broadcasted_iota(
                        jnp.int32, (256, 256), 1
                    )
                    tile = jnp.where(cid >= rid, tile, 0.0)
                gram[rows, lanes] = tile

    steps = {
        "attention_z": attention_z, "attention_y": attention_y, "project": project, "combine": combine,
        "squares": squares, "norm": norm, "columns_x": columns_x, "rows_z": rows_z,
        "rows_y": rows_y, "rows_core": rows_core, "gram": gram_part,
    }
    order = sorted(
        (start + pitch * c, c, name) for name, start, pitch in STEPS for c in range(PARTS)
    )
    for _, c, name in order:
        steps[name](c)

    arrived(SR, ks.at[3], kr.at[3])
    stream[pl.ds(off_mine, 64), :] = S2[k]
    stream[pl.ds(off_other, 64), :] = SR[...]
    for c, when in sends:
        if when is None:
            c.wait_send()
        else:
            pl.when(when)(c.wait_send)
    for c in range(PARTS):
        for d in range(4):
            yp = (y + 4 - d) % 4
            pl.when(yp != x)(to_x(c, yp).wait_send)
            if d:
                to_zl(c, (zl + d) % 4).wait_send()


def local(attn, w_out, resid, gain):
    dma = pltpu.SemaphoreType.DMA
    vmem = pltpu.VMEM
    whole = pl.BlockSpec(memory_space=pltpu.VMEM)
    anywhere = pl.BlockSpec(memory_space=pl.ANY)
    parts, sixteen = dma((PARTS, 4)), dma((PARTS, 16))
    return pl.pallas_call(
        kernel,
        out_shape=(
            jax.ShapeDtypeStruct((128, 512), BF16),
            jax.ShapeDtypeStruct((1024, 512), F32),
        ),
        in_specs=[anywhere] * 4,
        out_specs=(whole, whole),
        scratch_shapes=[
            vmem((PARTS, 4, 4, T, 1024), BF16),
            vmem((2, 1024, 512), BF16),
            vmem((PARTS, 4, 4, T, 1024), BF16),
            vmem((PARTS, 4, 4, T, 1024), BF16),
            vmem((PARTS, 4, T, 1024), F32),
            vmem((PARTS, 4, T, 1024), BF16),
            vmem((PARTS, 4, T, 1024), BF16),
            vmem((2, 64, 512), BF16),
            vmem((2, 1, 512), F32),
            vmem((PARTS, T, 1024), F32),
            vmem((2, 64, 512), BF16),
            vmem((64, 512), BF16),
            vmem((PARTS, 1, 128), F32),
            vmem((PARTS, 16, 1, 128), F32),
            vmem((PARTS, 4, T, 256), BF16),
            vmem((PARTS, 4, 4, 4, T, 256), BF16),
            vmem((PARTS, 4, 4, 2, T, 256), BF16),
            vmem((2, PARTS, 4, 4, 4, T, 256), BF16),
            dma((3 + PARTS,)), dma((4,)), dma((4,)),
            parts, parts, parts, parts, parts, parts, parts, parts,
            sixteen, sixteen, parts, parts, sixteen, sixteen,
            parts, parts, parts, parts, parts, parts,
            dma((PARTS,)), dma((PARTS,)), parts, parts,
        ],
        compiler_params=pltpu.CompilerParams(
            collective_id=0, has_side_effects=True, vmem_limit_bytes=40 << 20
        ),
        cost_estimate=pl.CostEstimate(
            flops=4 * 2048 * 1024 * 512, bytes_accessed=16 << 20, transcendentals=128
        ),
    )(attn, w_out, resid, gain.reshape(1, 512))


def solution(mesh):
    placed = (P("col", "row"), P("row", "col"), P("row", "col"), P("col"))
    return jax.shard_map(
        local,
        mesh=mesh,
        in_specs=placed,
        out_specs=(P("row", "col"), P("row", "col")),
        check_vma=False,
    )
```
